512 devices in a mesh: dp: 32 (over z_lo, x, core), fsdp: 16 (over y, z_hi).
Axes of the slice: x: 4, y: 4, z: 16 (z_hi: 4, z_lo: 4; z = z_hi * 4 + z_lo), core: 2. Of those that a mesh axis runs over, the one named last changes fastest.
Arguments:
- activations: bfloat16 [8192, 8192], P('dp', 'fsdp'), may hold values from -6 to 6
- out_cotangent: bfloat16 [8192, 28672], P('dp', 'fsdp'), may hold values from -6 to 6
- projector: bfloat16 [8192, 512], P('fsdp'), may hold values from -0.0625 to 0.0625
- first_moment: float32 [512, 28672], P('dp', 'fsdp'), may hold values from -4 to 4
- second_moment: float32 [512, 28672], P('dp', 'fsdp'), may hold values from 0.05 to 2
Outputs:
- new_first: float32 [512, 28672], P('dp', 'fsdp')
- new_second: float32 [512, 28672], P('dp', 'fsdp')
- weight_update: bfloat16 [28672, 8192], P('fsdp', 'dp')
The draws below stay inside these ranges and needn't reach their ends.
All inputs are finite; a program needn't handle non-finite values.
Results may differ from the reference program's by a relative error of at most 0.017.
Values may be sent and summed in bfloat16 or wider, within the bound.
A program may use at most 64 MiB of HBM per device.

```python
import math
import jax
import jax.numpy as jnp
from jax import lax

D = 8192
FF = 28672
R = 512
STEP = 100
TOKENS = 8192
N_FSDP = 16


def levels(stream_key, shape, split, low, top_value):
    def one(dim, shards_of):
        heights = jax.random.uniform(jax.random.fold_in(jax.random.fold_in(stream_key, 6), dim), (shards_of,), jnp.float32, low / len(split), top_value / len(split))
        return jnp.repeat(jnp.exp(heights), shape[dim] // shards_of).reshape((-1,) + (1,) * (len(shape) - dim - 1))

    level = one(*split[0])
    for cut in split[1:]:
        level = level * one(*cut)
    return level


def normal_values(key, dims, spread, bound, shards=(), kind=jnp.bfloat16):
    loudness = levels(key, dims, shards, -0.22, 0.18) if shards else 1.0
    drawn = jax.random.normal(key, dims, jnp.float32) * spread * loudness
    return jnp.minimum(jnp.maximum(drawn, -bound), bound).astype(kind)


def setup_inputs(seed: int = 0) -> dict:
    splits = jax.random.split(jax.random.key(seed), 6)
    return {
        "activations": normal_values(splits[0], (TOKENS, D), 1.0, 6.0, ((0, 32), (1, 16))),
        "out_cotangent": normal_values(splits[1], (TOKENS, FF), 1.0, 6.0, ((0, 32), (1, 16))),
        "projector": normal_values(splits[2], (D, R), D ** -0.5, 0.0625, ((0, 16),)),
        "first_moment": normal_values(splits[3], (R, FF), 0.5, 4.0, ((0, 32), (1, 16)), jnp.float32),
        "second_moment": jnp.clip(jnp.exp(math.log(2.0) - 3.6888794 * jax.random.uniform(splits[4], (R, FF), jnp.float32) ** levels(splits[4], (R, FF), ((0, 32), (1, 16)), -0.2, 0.2)), 0.05, 2.0),
    }


def adam_update(lowgrad, first_moment, second_moment):
    new_first = 0.9 * first_moment + (1.0 - 0.9) * lowgrad
    new_second = 0.999 * second_moment + (1.0 - 0.999) * lowgrad * lowgrad
    first_fix = 1.0 - 0.9 ** STEP
    second_fix = 1.0 - 0.999 ** STEP
    direction = (new_first / first_fix / (jnp.sqrt(new_second / second_fix) + 1e-08)).astype(jnp.bfloat16)
    return (new_first, new_second, direction)

def reference(activations, out_cotangent, projector, first_moment, second_moment):
    projected = jnp.dot(activations, projector, preferred_element_type=jnp.float32).astype(jnp.bfloat16)
    block_width = FF // N_FSDP
    block_ids = jnp.arange(N_FSDP, dtype=jnp.int32)

    def grad_block(block_index):
        columns = lax.dynamic_slice_in_dim(out_cotangent, block_index * block_width, block_width, 1)
        return lax.dot_general(projected, columns, (((0,), (0,)), ((), ())), preferred_element_type=jnp.float32)
    pieces = lax.map(grad_block, block_ids)
    lowgrad = jnp.transpose(pieces, (1, 0, 2)).reshape(R, FF) * (1.0 / math.sqrt(TOKENS))
    new_first, new_second, direction = adam_update(lowgrad, first_moment, second_moment)

    def update_block(block_index):
        row_block = lax.dynamic_slice_in_dim(direction, block_index * block_width, block_width, 1)
        product = lax.dot_general(row_block, projector, (((0,), (1,)), ((), ())), preferred_element_type=jnp.float32)
        return product.astype(jnp.bfloat16)
    weight_update = lax.map(update_block, block_ids).reshape(FF, D)
    return (new_first, new_second, weight_update)
```

```python
import functools
import math

import jax
import jax.numpy as jnp
from jax import lax
from jax.experimental import pallas as pl
from jax.experimental.pallas import tpu as pltpu
from jax.sharding import PartitionSpec as P

MESH = pl.DeviceIdType.MESH
STEP = 100
BF = jnp.bfloat16
F32 = jnp.float32
CHUNKS = ((0, 256), (256, 256), (512, 384))
N = 4


def adam(lowgrad, first, second):
    new_first = 0.9 * first + (1.0 - 0.9) * lowgrad
    new_second = 0.999 * second + (1.0 - 0.999) * lowgrad * lowgrad
    first_fix = 1.0 - 0.9**STEP
    second_fix = 1.0 - 0.999**STEP
    direction = new_first / first_fix / (jnp.sqrt(new_second / second_fix) + 1e-08)
    return new_first, new_second, direction.astype(BF)


def kernel(
    grad_scale, act_ref, cot_ref, proj_ref, m1_ref, m2_ref,
    nf_ref, ns_ref, up_ref,
    act, proj, cot_own, cot_sib, mom1, mom2, basis,
    part, y_in, y_sum, z_in, pj, pj_sib,
    lg, opp_l, opp_r, a_l, a_r, b_l, b_r, s2, zl_in,
    new1, new2, dirs, dirs_sib, upd,
    send_sems, recv_sems, local_sems,
):
    dp, fs = lax.axis_index("dp"), lax.axis_index("fsdp")
    zl, x, c = dp // 8, (dp // 2) % 4, dp % 2
    y, zh = fs // 4, fs % 4
    half = cot_own.shape[1]

    def dev(x=x, y=y, zh=zh, zl=zl, c=c):
        return (zl * 8 + x * 2 + c, y * 4 + zh)

    def at(base, off):
        return lax.rem(base + off, N)

    sibling = dev(c=1 - c)
    partner = dev(x=zh, y=zl, zh=x, zl=y)
    is_self = jnp.logical_and(x == zh, y == zl)
    counter = [0, 0]
    sent = []

    def remote(src, dst, device):
        i = counter[0]
        counter[0] += 1
        copy = pltpu.make_async_remote_copy(
            src_ref=src, dst_ref=dst, send_sem=send_sems.at[i], recv_sem=recv_sems.at[i],
            device_id=device, device_id_type=MESH,
        )
        return copy

    def go(src, dst, device):
        copy = remote(src, dst, device)
        copy.start()
        sent.append(copy)
        return copy

    def fetch(src, dst):
        i = counter[1]
        counter[1] += 1
        copy = pltpu.make_async_copy(src, dst, local_sems.at[i])
        copy.start()
        return copy

    own_cols = pl.ds(pl.multiple_of(c * half, 128), half)
    sib_cols = pl.ds(pl.multiple_of((1 - c) * half, 128), half)

    barrier = pltpu.get_barrier_semaphore()
    peers = [sibling]
    for o in (1, 2, 3):
        peers += [dev(y=at(y, o)), dev(zh=at(zh, o)), dev(x=at(x, o)), dev(zl=at(zl, o))]
    get_act = fetch(act_ref, act)
    get_proj = fetch(proj_ref, proj)
    for p in peers:
        pl.semaphore_signal(barrier, inc=1, device_id=p, device_id_type=MESH)

    @pl.when(jnp.logical_not(is_self))
    def _():
        pl.semaphore_signal(barrier, inc=1, device_id=partner, device_id_type=MESH)

    get_cot = fetch(cot_ref.at[:, own_cols], cot_own)
    get_m1 = fetch(m1_ref.at[:, own_cols], mom1.at[c])
    get_m2 = fetch(m2_ref.at[:, own_cols], mom2.at[c])

    get_act.wait()
    get_proj.wait()
    partial = jnp.dot(act[...], proj[...], preferred_element_type=F32)
    part[...] = jnp.transpose(partial).astype(BF).reshape(part.shape)

    pl.semaphore_wait(barrier, jnp.where(is_self, len(peers), len(peers) + 1))

    ys = [go(part.at[at(y, o)], y_in.at[o - 1], dev(y=at(y, o))) for o in (1, 2, 3)]
    cot_x = go(cot_ref.at[:, sib_cols], cot_sib, sibling)
    m1_x = go(m1_ref.at[:, sib_cols], mom1.at[c], sibling)
    m2_x = go(m2_ref.at[:, sib_cols], mom2.at[c], sibling)
    total = part[y].astype(F32)
    for o, copy in enumerate(ys):
        copy.wait_recv()
        total += y_in[o].astype(F32)
    y_sum[...] = total.astype(BF)
    zs = [go(y_sum.at[at(zh, o)], z_in.at[o - 1], dev(zh=at(zh, o))) for o in (1, 2, 3)]
    total = y_sum[zh].astype(F32)
    for o, copy in enumerate(zs):
        copy.wait_recv()
        total += z_in[o].astype(F32)
    pj[y, zh] = total.astype(BF)

    zg = [go(pj.at[y, zh], pj.at[y, zh], dev(zh=at(zh, o))) for o in (1, 2, 3)]
    for copy in zg:
        copy.wait_recv()
    yg = [go(pj.at[y], pj.at[y], dev(y=at(y, o))) for o in (1, 2, 3)]
    sib = [go(pj.at[y], pj_sib.at[y], sibling)]
    piece = basis.shape[1]
    rows = pl.ds(pl.multiple_of(c * (N * piece) + zl * piece, piece), piece)
    basis_x = remote(proj_ref.at[rows], basis.at[zl], partner)
    basis_own = pltpu.make_async_copy(proj_ref.at[rows], basis.at[zl], local_sems.at[counter[1]])
    counter[1] += 1

    @pl.when(is_self)
    def _():
        basis_own.start()

    @pl.when(jnp.logical_not(is_self))
    def _():
        basis_x.start()

    for o, copy in zip((1, 2, 3), yg):
        copy.wait_recv()
        yy = at(y, N - o)
        sib.append(go(pj.at[yy], pj_sib.at[yy], sibling))
    get_cot.wait()
    cot_x.wait_recv()
    for copy in sib:
        copy.wait_recv()

    right, left = at(x, 1), at(x, 3)
    opposite = at(x, 2)
    to_right, to_left = dev(x=right), dev(x=left)
    low, high = pl.ds(0, 2), pl.ds(2, 2)
    flight = [dict() for _ in CHUNKS]

    def produce(k):
        start, width = CHUNKS[k]
        cols = pl.ds(start, width)
        f = flight[k]
        grad = jnp.dot(
            pj[...].reshape(N * N * 32, -1), cot_own[:, cols], preferred_element_type=F32
        ) + jnp.dot(
            pj_sib[...].reshape(N * N * 32, -1), cot_sib[:, cols], preferred_element_type=F32
        )
        lg[:, :, :, cols] = grad.astype(BF).reshape(N, N, 32, width)
        f["opp_l"] = go(lg.at[low, opposite, :, cols], opp_l.at[:, :, cols], to_right)
        f["opp_r"] = go(lg.at[high, opposite, :, cols], opp_r.at[:, :, cols], to_left)
        f["b_l"] = go(lg.at[high, right, :, cols], b_l.at[:, :, cols], to_right)
        f["a_r"] = go(lg.at[low, left, :, cols], a_r.at[:, :, cols], to_left)

    def pass_on(k):
        start, width = CHUNKS[k]
        cols = pl.ds(start, width)
        f = flight[k]
        f["opp_l"].wait_recv()
        lg[0:2, right, :, cols] = (
            lg[0:2, right, :, cols].astype(F32) + opp_l[:, :, cols].astype(F32)
        ).astype(BF)
        f["a_l"] = go(lg.at[low, right, :, cols], a_l.at[:, :, cols], to_right)
        f["opp_r"].wait_recv()
        lg[2:4, left, :, cols] = (
            lg[2:4, left, :, cols].astype(F32) + opp_r[:, :, cols].astype(F32)
        ).astype(BF)
        f["b_r"] = go(lg.at[high, left, :, cols], b_r.at[:, :, cols], to_left)

    def sum_x(k):
        start, width = CHUNKS[k]
        cols = pl.ds(start, width)
        f = flight[k]
        f["a_l"].wait_recv()
        f["a_r"].wait_recv()
        s2[0:2, :, cols] = (
            lg[0:2, x, :, cols].astype(F32) + a_l[:, :, cols].astype(F32)
            + a_r[:, :, cols].astype(F32)
        ).astype(BF)
        f["b_l"].wait_recv()
        f["b_r"].wait_recv()
        s2[2:4, :, cols] = (
            lg[2:4, x, :, cols].astype(F32) + b_l[:, :, cols].astype(F32)
            + b_r[:, :, cols].astype(F32)
        ).astype(BF)
        f["zl"] = [
            go(s2.at[at(zl, o), :, cols], zl_in.at[o - 1, :, cols], dev(zl=at(zl, o)))
            for o in (1, 2, 3)
        ]

    def step(k):
        start, width = CHUNKS[k]
        cols = pl.ds(start, width)
        f = flight[k]
        if k == 0:
            get_m1.wait()
            get_m2.wait()
            m1_x.wait_recv()
            m2_x.wait_recv()
        total = s2[zl, :, cols].astype(F32)
        for o, copy in enumerate(f["zl"]):
            copy.wait_recv()
            total += zl_in[o, :, cols].astype(F32)
        lowgrad = (total * grad_scale).reshape(2, 16, width)
        first, second, direction = adam(lowgrad, mom1[:, :, cols], mom2[:, :, cols])
        dirs[zl, x, :, cols] = direction.reshape(32, width)
        f["zg"] = [
            go(dirs.at[zl, x, :, cols], dirs.at[zl, x, :, cols], dev(zl=at(zl, o)))
            for o in (1, 2, 3)
        ]
        new1[:, :, cols] = first
        new2[:, :, cols] = second

    def send_x(k):
        start, width = CHUNKS[k]
        cols = pl.ds(start, width)
        f = flight[k]
        for copy in f["zg"]:
            copy.wait_recv()
        src_a, src_b = dirs.at[low, x, :, cols], dirs.at[high, x, :, cols]
        f["ga_l"] = go(src_a, src_a, to_right)
        f["gb_r"] = go(src_b, src_b, to_left)
        f["gb_l"] = go(src_b, src_b, to_right)
        f["ga_r"] = go(src_a, src_a, to_left)
        every = pl.ds(0, N)
        f["sib"] = [go(dirs.at[every, x, :, cols], dirs_sib.at[every, x, :, cols], sibling)]

    def forward_x(k):
        start, width = CHUNKS[k]
        cols = pl.ds(start, width)
        f = flight[k]
        every = pl.ds(0, N)
        f["ga_l"].wait_recv()
        src = dirs.at[low, left, :, cols]
        f["oa"] = go(src, src, to_right)
        f["gb_r"].wait_recv()
        src = dirs.at[high, right, :, cols]
        f["ob"] = go(src, src, to_left)
        f["gb_l"].wait_recv()
        f["sib"].append(
            go(dirs.at[every, left, :, cols], dirs_sib.at[every, left, :, cols], sibling)
        )
        f["ga_r"].wait_recv()
        f["sib"].append(
            go(dirs.at[every, right, :, cols], dirs_sib.at[every, right, :, cols], sibling)
        )

    def last_x(k):
        start, width = CHUNKS[k]
        cols = pl.ds(start, width)
        f = flight[k]
        every = pl.ds(0, N)
        f["oa"].wait_recv()
        f["ob"].wait_recv()
        f["sib"].append(
            go(dirs.at[every, opposite, :, cols], dirs_sib.at[every, opposite, :, cols], sibling)
        )

    back = (((0,), (1,)), ((), ()))
    written = []

    def update(k):
        start, width = CHUNKS[k]
        cols = pl.ds(start, width)
        f = flight[k]
        whole = basis[...].reshape(N * piece, -1)
        for j, (ref, core) in enumerate(((dirs, c), (dirs_sib, 1 - c))):
            if j == 1:
                for copy in f["sib"]:
                    copy.wait_recv()
            d = ref[:, :, :, cols].reshape(N * N * 32, width)
            upd[j, cols] = lax.dot_general(
                d, whole, back, preferred_element_type=F32
            ).astype(BF)
            written.append(
                fetch(
                    upd.at[j, cols],
                    up_ref.at[pl.ds(pl.multiple_of(core * half + start, 128), width)],
                )
            )

    def basis_round():
        @pl.when(is_self)
        def _():
            basis_own.wait()

        @pl.when(jnp.logical_not(is_self))
        def _():
            basis_x.wait_recv()

        return [go(basis.at[y], basis.at[y], dev(y=at(y, o))) for o in (1, 2, 3)]

    stages = (produce, pass_on, sum_x, step, send_x, forward_x, last_x, update)
    moments_out = None
    for t in range(len(CHUNKS) + len(stages) - 1):
        for s in reversed(range(len(stages))):
            k = t - s
            if 0 <= k < len(CHUNKS):
                if s == 2 and k == 0:
                    basis_copies = basis_round()
                if s == 7 and k == 0:
                    for copy in basis_copies:
                        copy.wait_recv()
                stages[s](k)
                if s == 3 and k == len(CHUNKS) - 1:
                    moments_out = [
                        go(new1.at[1 - c], nf_ref.at[:, own_cols], sibling),
                        go(new2.at[1 - c], ns_ref.at[:, own_cols], sibling),
                    ]
                    written.append(fetch(new1.at[c], nf_ref.at[:, own_cols]))
                    written.append(fetch(new2.at[c], ns_ref.at[:, own_cols]))
    for copy in moments_out:
        copy.wait_recv()
    for copy in written:
        copy.wait()
    for copy in sent:
        copy.wait_send()

    @pl.when(jnp.logical_not(is_self))
    def _():
        basis_x.wait_send()


def local(activations, out_cotangent, projector, first_moment, second_moment):
    tokens, features = activations.shape
    ff = out_cotangent.shape[1]
    rank = projector.shape[1]
    half = ff // 2
    total_tokens = tokens * lax.axis_size("dp")
    width = projector.shape[0] // 2
    block = (2, 32, half)
    remotes = 3 + 1 + 3 * 5 + 3 + 3 + 2 + len(CHUNKS) * (6 + 3 + 3 + 6 + 4)
    locals_ = 8 + 2 * len(CHUNKS)
    vmem = pltpu.VMEM
    scratch = [
        vmem((tokens, features), BF), vmem(projector.shape, BF),
        vmem((tokens, half), BF), vmem((tokens, half), BF),
        vmem((2, 16, half), F32), vmem((2, 16, half), F32),
        vmem((N, width // N, rank), BF),
        vmem((N, N, 32, tokens), BF), vmem((3, N, 32, tokens), BF), vmem((N, 32, tokens), BF),
        vmem((3, 32, tokens), BF), vmem((N, N, 32, tokens), BF), vmem((N, N, 32, tokens), BF),
        vmem((N, N, 32, half), BF),
        vmem(block, BF), vmem(block, BF), vmem(block, BF), vmem(block, BF),
        vmem(block, BF), vmem(block, BF),
        vmem((N, 32, half), BF), vmem((3, 32, half), BF),
        vmem((2, 16, half), F32), vmem((2, 16, half), F32),
        vmem((N, N, 32, half), BF), vmem((N, N, 32, half), BF),
        vmem((2, half, width), BF),
        pltpu.SemaphoreType.DMA((remotes,)), pltpu.SemaphoreType.DMA((remotes,)),
        pltpu.SemaphoreType.DMA((locals_,)),
    ]
    anyspec = pl.BlockSpec(memory_space=pl.ANY)
    return pl.pallas_call(
        functools.partial(kernel, 1.0 / math.sqrt(total_tokens)),
        out_shape=(
            jax.ShapeDtypeStruct(first_moment.shape, F32),
            jax.ShapeDtypeStruct(second_moment.shape, F32),
            jax.ShapeDtypeStruct((ff, width), BF),
        ),
        in_specs=[anyspec] * 5,
        out_specs=(anyspec,) * 3,
        scratch_shapes=scratch,
        compiler_params=pltpu.CompilerParams(
            collective_id=0, has_side_effects=True, vmem_limit_bytes=48 * 1024 * 1024
        ),
    )(activations, out_cotangent, projector, first_moment, second_moment)


def solution(mesh):
    placed = (P("dp", "fsdp"), P("dp", "fsdp"), P("fsdp", None), P("dp", "fsdp"), P("dp", "fsdp"))
    return jax.shard_map(
        local,
        mesh=mesh,
        in_specs=placed,
        out_specs=(P("dp", "fsdp"), P("dp", "fsdp"), P("fsdp", "dp")),
        check_vma=False,
    )
```

```python
import functools
import math

import jax
import jax.numpy as jnp
from jax import lax
from jax.experimental import pallas as pl
from jax.experimental.pallas import tpu as pltpu
from jax.sharding import PartitionSpec as P

MESH = pl.DeviceIdType.MESH
STEP = 100
BF = jnp.bfloat16
F32 = jnp.float32
CHUNKS = ((0, 256), (256, 256), (512, 384))
N = 4
ORDER = (2, 1, 3, 0)


def adam(lowgrad, first, second):
    new_first = 0.9 * first + (1.0 - 0.9) * lowgrad
    new_second = 0.999 * second + (1.0 - 0.999) * lowgrad * lowgrad
    first_fix = 1.0 - 0.9**STEP
    second_fix = 1.0 - 0.999**STEP
    direction = new_first / first_fix / (jnp.sqrt(new_second / second_fix) + 1e-08)
    return new_first, new_second, direction.astype(BF)


def kernel(
    grad_scale, act_ref, cot_ref, proj_ref, m1_ref, m2_ref,
    nf_ref, ns_ref, up_ref,
    act, proj, cot_own, cot_sib, mom1, mom2, basis, quarter, turned,
    part, y_in, y_sum, z_in, pj, pj_sib,
    lg, g_in, s2, zl_in, new1, new2, dirs, dirs_sib, upd,
    send_sems, recv_sems, local_sems,
):
    dp, fs = lax.axis_index("dp"), lax.axis_index("fsdp")
    zl, x, c = dp // 8, (dp // 2) % 4, dp % 2
    y, zh = fs // 4, fs % 4
    half = cot_own.shape[1]

    def dev(x=x, y=y, zh=zh, zl=zl, c=c):
        return (zl * 8 + x * 2 + c, y * 4 + zh)

    def at(base, off):
        return lax.rem(base + off, N)

    sibling = dev(c=1 - c)
    root = y == zl
    turn = at(x, zl)
    goal = lax.rem(zh - x - zl + 2 * N, N)
    turns, moves = turn != 0, goal != x
    counter = [0, 0]
    sent = []

    def remote(src, dst, device, recv=None):
        i = counter[0]
        counter[0] += 1
        copy = pltpu.make_async_remote_copy(
            src_ref=src, dst_ref=dst, send_sem=send_sems.at[i],
            recv_sem=recv_sems.at[i if recv is None else recv],
            device_id=device, device_id_type=MESH,
        )
        return copy

    def go(src, dst, device):
        copy = remote(src, dst, device)
        copy.start()
        sent.append(copy)
        return copy

    def held(src, dst):
        i = counter[1]
        counter[1] += 1
        return pltpu.make_async_copy(src, dst, local_sems.at[i])

    def fetch(src, dst):
        copy = held(src, dst)
        copy.start()
        return copy

    own_cols = pl.ds(pl.multiple_of(c * half, 128), half)
    sib_cols = pl.ds(pl.multiple_of((1 - c) * half, 128), half)

    barrier = pltpu.get_barrier_semaphore()
    peers = [sibling]
    for o in (1, 2, 3):
        peers += [dev(y=at(y, o)), dev(zh=at(zh, o)), dev(x=at(x, o)), dev(zl=at(zl, o))]
    get_act = fetch(act_ref, act)
    get_proj = fetch(proj_ref, proj)
    for p in peers:
        pl.semaphore_signal(barrier, inc=1, device_id=p, device_id_type=MESH)

    get_cot = fetch(cot_ref.at[:, own_cols], cot_own)
    get_m1 = fetch(m1_ref.at[:, own_cols], mom1.at[c])
    get_m2 = fetch(m2_ref.at[:, own_cols], mom2.at[c])

    get_act.wait()
    get_proj.wait()
    partial = jnp.dot(act[...], proj[...], preferred_element_type=F32)
    part[...] = jnp.transpose(partial).astype(BF).reshape(part.shape)

    pl.semaphore_wait(barrier, len(peers))
    pieces = [at(x, o) for o in ORDER]
    ys = [
        [go(part.at[at(y, o), p], y_in.at[o - 1, p], dev(y=at(y, o))) for o in (2, 1, 3)]
        for p in pieces
    ]
    cot_x = go(cot_ref.at[:, sib_cols], cot_sib, sibling)
    m1_x = go(m1_ref.at[:, sib_cols], mom1.at[c], sibling)
    m2_x = go(m2_ref.at[:, sib_cols], mom2.at[c], sibling)
    zs = []
    for p, copies in zip(pieces, ys):
        for copy in copies:
            copy.wait_recv()
        total = part[y, p].astype(F32)
        for o in range(3):
            total += y_in[o, p].astype(F32)
        y_sum[p] = total.astype(BF)
        zs.append(
            [go(y_sum.at[p], z_in.at[o - 1, p], dev(zh=at(zh, o))) for o in (2, 1, 3)]
        )

    piece = basis.shape[1]

    def rows(q):
        return proj_ref.at[pl.ds(pl.multiple_of(c * (N * piece) + q * piece, piece), piece)]

    first_sem = counter[0]
    basis_cut = [
        remote(rows(at(y, o)), quarter, dev(y=at(y, o)), first_sem) for o in (1, 2, 3)
    ]
    basis_own = held(rows(y), quarter)

    @pl.when(root)
    def _():
        for basis_part in basis_cut:
            basis_part.start()
        basis_own.start()

    handed = [None] * N
    relayed = [None] * N
    grads = [[] for _ in CHUNKS]

    def add_z(i):
        p = pieces[i]
        for copy in zs[i]:
            copy.wait_recv()
        total = y_sum[p].astype(F32)
        for o in range(3):
            total += z_in[o, p].astype(F32)
        pj[y, p] = total.astype(BF)
        handed[i] = [go(pj.at[y, p], pj.at[y, p], dev(y=at(y, o))) for o in (2, 1, 3)]
        relayed[i] = [go(pj.at[y, p], pj_sib.at[y, p], sibling)]

    def relay(i):
        p = pieces[i]
        for o, copy in zip((2, 1, 3), handed[i]):
            copy.wait_recv()
            yy = at(y, N - o)
            relayed[i].append(go(pj.at[yy, p], pj_sib.at[yy, p], sibling))

    def multiply(i):
        p, o = pieces[i], ORDER[i]
        if i == 0:
            get_cot.wait()
            cot_x.wait_recv()
        for copy in relayed[i]:
            copy.wait_recv()
        grad = jnp.dot(
            pj[:, p].reshape(N * 32, -1), cot_own[...], preferred_element_type=F32
        ) + jnp.dot(pj_sib[:, p].reshape(N * 32, -1), cot_sib[...], preferred_element_type=F32)
        lg[p] = grad.astype(BF).reshape(N, 32, half)
        if o:
            for k, (start, width) in enumerate(CHUNKS):
                cols = pl.ds(start, width)
                grads[k].append(
                    go(lg.at[p, :, :, cols], g_in.at[o - 1, :, :, cols], dev(x=p))
                )

    basis_turn = remote(quarter, turned, dev(zh=at(zh, turn)))
    basis_stay = held(quarter, turned)
    basis_move = remote(turned, basis.at[y], dev(x=goal))
    basis_keep = held(turned, basis.at[y])

    def turn_basis(i):
        @pl.when(root)
        def _():
            basis_own.wait()

        @pl.when(jnp.logical_not(root))
        def _():
            basis_cut[0].wait_recv()

        @pl.when(turns)
        def _():
            basis_turn.start()

        @pl.when(jnp.logical_not(turns))
        def _():
            basis_stay.start()

    def move_basis():
        @pl.when(turns)
        def _():
            basis_turn.wait_recv()

        @pl.when(jnp.logical_not(turns))
        def _():
            basis_stay.wait()

        @pl.when(moves)
        def _():
            basis_move.start()

        @pl.when(jnp.logical_not(moves))
        def _():
            basis_keep.start()

    def share_basis():
        @pl.when(moves)
        def _():
            basis_move.wait_recv()

        @pl.when(jnp.logical_not(moves))
        def _():
            basis_keep.wait()

        return [go(basis.at[y], basis.at[y], dev(y=at(y, o))) for o in (1, 2, 3)]

    for act_on, i in (
        (add_z, 0), (add_z, 1), (relay, 0), (multiply, 0), (add_z, 2), (relay, 1), (multiply, 1),
        (add_z, 3), (turn_basis, 0), (relay, 2), (multiply, 2), (relay, 3), (multiply, 3),
    ):
        act_on(i)

    flight = [dict() for _ in CHUNKS]

    def sum_x(k):
        start, width = CHUNKS[k]
        cols = pl.ds(start, width)
        for copy in grads[k]:
            copy.wait_recv()
        total = lg[x, :, :, cols].astype(F32)
        for o in range(3):
            total += g_in[o, :, :, cols].astype(F32)
        s2[:, :, cols] = total.astype(BF)
        flight[k]["zl"] = [
            go(s2.at[at(zl, o), :, cols], zl_in.at[o - 1, :, cols], dev(zl=at(zl, o)))
            for o in (1, 2, 3)
        ]

    def step(k):
        start, width = CHUNKS[k]
        cols = pl.ds(start, width)
        f = flight[k]
        if k == 0:
            get_m1.wait()
            get_m2.wait()
            m1_x.wait_recv()
            m2_x.wait_recv()
        for copy in f["zl"]:
            copy.wait_recv()
        total = s2[zl, :, cols].astype(F32)
        for o in range(3):
            total += zl_in[o, :, cols].astype(F32)
        lowgrad = (total * grad_scale).reshape(2, 16, width)
        first, second, direction = adam(lowgrad, mom1[:, :, cols], mom2[:, :, cols])
        dirs[zl, x, :, cols] = direction.reshape(32, width)
        src = dirs.at[zl, x, :, cols]
        f["zg"] = [go(src, src, dev(zl=at(zl, o))) for o in (1, 2, 3)]
        new1[:, :, cols] = first
        new2[:, :, cols] = second

    def block(ref, k, p):
        start, width = CHUNKS[k]
        return ref.at[pl.ds(0, N), p, :, pl.ds(start, width)]

    def send_x(k):
        f = flight[k]
        for copy in f["zg"]:
            copy.wait_recv()
        src = block(dirs, k, x)
        f["xg"] = [go(src, src, dev(x=at(x, o))) for o in (2, 1, 3)]
        f["sib"] = [go(src, block(dirs_sib, k, x), sibling)]

    def relay_x(k):
        f = flight[k]
        for o, copy in zip((2, 1, 3), f["xg"]):
            copy.wait_recv()
            xx = at(x, N - o)
            f["sib"].append(go(block(dirs, k, xx), block(dirs_sib, k, xx), sibling))

    back = (((0,), (1,)), ((), ()))
    written = []

    def update(k):
        start, width = CHUNKS[k]
        cols = pl.ds(start, width)
        if k == 0:
            for copy in basis_copies:
                copy.wait_recv()
        whole = basis[...].reshape(N * piece, -1)
        for j, (ref, core) in enumerate(((dirs, c), (dirs_sib, 1 - c))):
            if j == 1:
                for copy in flight[k]["sib"]:
                    copy.wait_recv()
            d = ref[:, :, :, cols].reshape(N * N * 32, width)
            upd[j, cols] = lax.dot_general(
                d, whole, back, preferred_element_type=F32
            ).astype(BF)
            written.append(
                fetch(
                    upd.at[j, cols],
                    up_ref.at[pl.ds(pl.multiple_of(core * half + start, 128), width)],
                )
            )

    def each(act_on):
        for k in range(len(CHUNKS)):
            act_on(k)

    each(sum_x)
    move_basis()
    each(step)
    moments_out = [
        go(new1.at[1 - c], nf_ref.at[:, own_cols], sibling),
        go(new2.at[1 - c], ns_ref.at[:, own_cols], sibling),
    ]
    written.append(fetch(new1.at[c], nf_ref.at[:, own_cols]))
    written.append(fetch(new2.at[c], ns_ref.at[:, own_cols]))
    send_x(0)
    basis_copies = share_basis()
    for k in range(1, len(CHUNKS)):
        send_x(k)
    for k in range(len(CHUNKS)):
        relay_x(k)
        update(k)
    assert counter[0] <= send_sems.shape[0] and counter[1] <= local_sems.shape[0]
    for copy in moments_out:
        copy.wait_recv()
    for copy in written:
        copy.wait()
    for copy in sent:
        copy.wait_send()

    @pl.when(root)
    def _():
        for basis_part in basis_cut:
            basis_part.wait_send()

    @pl.when(turns)
    def _():
        basis_turn.wait_send()

    @pl.when(moves)
    def _():
        basis_move.wait_send()


def hand_over(a_ref, b_ref, c_ref, a_out, b_out, c_out, a, b, c, sems):
    rows = c.shape[0] // 4
    trips = [(a_ref, a, a_out), (b_ref, b, b_out)]
    for i in range(4):
        part = pl.ds(i * rows, rows)
        trips.append((c_ref.at[part], c.at[part], c_out.at[part]))
    inward = [pltpu.make_async_copy(s, v, sems.at[0, i]) for i, (s, v, _) in enumerate(trips)]
    outward = [pltpu.make_async_copy(v, d, sems.at[1, i]) for i, (_, v, d) in enumerate(trips)]
    for copy in inward:
        copy.start()
    for arrive, leave in zip(inward, outward):
        arrive.wait()
        leave.start()
    for copy in outward:
        copy.wait()


def local(activations, out_cotangent, projector, first_moment, second_moment):
    tokens, features = activations.shape
    ff = out_cotangent.shape[1]
    rank = projector.shape[1]
    half = ff // 2
    width = projector.shape[0] // 2
    total_tokens = tokens * lax.axis_size("dp")
    remotes = 12 + 3 + 12 + N * 7 + 8 + len(CHUNKS) * (3 + 3 + 3 + 3 + 4) + 2
    locals_ = 10 + 2 * len(CHUNKS)
    vmem = pltpu.VMEM
    scratch = [
        vmem((tokens, features), BF), vmem(projector.shape, BF),
        vmem((tokens, half), BF), vmem((tokens, half), BF),
        vmem((2, 16, half), F32), vmem((2, 16, half), F32),
        vmem((N, width // N, rank), BF), vmem((width // N, rank), BF), vmem((width // N, rank), BF),
        vmem((N, N, 32, tokens), BF), vmem((3, N, 32, tokens), BF), vmem((N, 32, tokens), BF),
        vmem((3, N, 32, tokens), BF), vmem((N, N, 32, tokens), BF), vmem((N, N, 32, tokens), BF),
        vmem((N, N, 32, half), BF), vmem((3, N, 32, half), BF),
        vmem((N, 32, half), BF), vmem((3, 32, half), BF),
        vmem((2, 16, half), F32), vmem((2, 16, half), F32),
        vmem((N, N, 32, half), BF), vmem((N, N, 32, half), BF),
        vmem((2, half, width), BF),
        pltpu.SemaphoreType.DMA((remotes,)), pltpu.SemaphoreType.DMA((remotes,)),
        pltpu.SemaphoreType.DMA((locals_,)),
    ]
    anyspec = pl.BlockSpec(memory_space=pl.ANY)
    outs = (
        jax.ShapeDtypeStruct(first_moment.shape, F32),
        jax.ShapeDtypeStruct(second_moment.shape, F32),
        jax.ShapeDtypeStruct((ff, width), BF),
    )
    results = pl.pallas_call(
        functools.partial(kernel, 1.0 / math.sqrt(total_tokens)),
        out_shape=outs,
        in_specs=[anyspec] * 5,
        out_specs=(anyspec,) * 3,
        scratch_shapes=scratch,
        compiler_params=pltpu.CompilerParams(
            collective_id=0, has_side_effects=True, vmem_limit_bytes=56 * 1024 * 1024
        ),
    )(activations, out_cotangent, projector, first_moment, second_moment)
    return pl.pallas_call(
        hand_over,
        out_shape=outs,
        in_specs=[anyspec] * 3,
        out_specs=(anyspec,) * 3,
        scratch_shapes=[vmem(o.shape, o.dtype) for o in outs]
        + [pltpu.SemaphoreType.DMA((2, 6))],
        compiler_params=pltpu.CompilerParams(vmem_limit_bytes=56 * 1024 * 1024),
    )(*results)


def solution(mesh):
    placed = (P("dp", "fsdp"), P("dp", "fsdp"), P("fsdp", None), P("dp", "fsdp"), P("dp", "fsdp"))
    return jax.shard_map(
        local,
        mesh=mesh,
        in_specs=placed,
        out_specs=(P("dp", "fsdp"), P("dp", "fsdp"), P("fsdp", "dp")),
        check_vma=False,
    )
```

```python
import functools
import math

import jax
import jax.numpy as jnp
from jax import lax
from jax.experimental import pallas as pl
from jax.experimental.pallas import tpu as pltpu
from jax.sharding import PartitionSpec as P

MESH = pl.DeviceIdType.MESH
STEP = 100
BF = jnp.bfloat16
F32 = jnp.float32
CHUNKS = ((0, 256), (256, 256), (512, 384))
N = 4
PIECES = ((2, 0, 32), (1, 0, 32), (3, 0, 32), (0, 0, 32))
DIRECT = (0, 1, 2)


def adam(lowgrad, first, second):
    new_first = 0.9 * first + (1.0 - 0.9) * lowgrad
    new_second = 0.999 * second + (1.0 - 0.999) * lowgrad * lowgrad
    first_fix = 1.0 - 0.9**STEP
    second_fix = 1.0 - 0.999**STEP
    direction = new_first / first_fix / (jnp.sqrt(new_second / second_fix) + 1e-08)
    return new_first, new_second, direction.astype(BF)


def kernel(
    grad_scale, act_ref, cot_ref, proj_ref, m1_ref, m2_ref,
    nf_ref, ns_ref, up_ref,
    act, proj, cot_own, cot_sib, mom1, mom2, basis, quarter, turned,
    part, y_in, y_sum, z_in, pj, pj_sib,
    lg, g_in, s2, zl_in, new1, new2, dirs, dirs_sib, upd,
    send_sems, recv_sems, local_sems, opposite_in,
):
    dp, fs = lax.axis_index("dp"), lax.axis_index("fsdp")
    zl, x, c = dp // 8, (dp // 2) % 4, dp % 2
    y, zh = fs // 4, fs % 4
    half = cot_own.shape[1]

    def dev(x=x, y=y, zh=zh, zl=zl, c=c):
        return (zl * 8 + x * 2 + c, y * 4 + zh)

    def at(base, off):
        return lax.rem(base + off, N)

    sibling = dev(c=1 - c)
    root = y == zl
    turn = at(x, zl)
    goal = lax.rem(zh - x - zl + 2 * N, N)
    turns, moves = turn != 0, goal != x
    counter = [0, 0]
    sent = []

    def remote(src, dst, device, recv=None):
        i = counter[0]
        counter[0] += 1
        copy = pltpu.make_async_remote_copy(
            src_ref=src, dst_ref=dst, send_sem=send_sems.at[i],
            recv_sem=recv_sems.at[i if recv is None else recv],
            device_id=device, device_id_type=MESH,
        )
        return copy

    def go(src, dst, device):
        copy = remote(src, dst, device)
        copy.start()
        sent.append(copy)
        return copy

    def held(src, dst):
        i = counter[1]
        counter[1] += 1
        return pltpu.make_async_copy(src, dst, local_sems.at[i])

    def fetch(src, dst):
        copy = held(src, dst)
        copy.start()
        return copy

    own_cols = pl.ds(pl.multiple_of(c * half, 128), half)
    sib_cols = pl.ds(pl.multiple_of((1 - c) * half, 128), half)

    barrier = pltpu.get_barrier_semaphore()
    far = (2, 1, 3)
    peers = [dev(zh=at(zh, o)) for o in (1, 3)] + [dev(y=at(y, o)) for o in far] + [sibling]
    peers += [dev(y=at(y, o), c=1 - c) for o in far]
    peers += [dev(zl=at(zl, o)) for o in far] + [dev(x=at(x, o)) for o in far]
    get_act = fetch(act_ref, act)
    get_proj = fetch(proj_ref, proj)
    for p in peers:
        pl.semaphore_signal(barrier, inc=1, device_id=p, device_id_type=MESH)

    get_cot = fetch(cot_ref.at[:, own_cols], cot_own)
    get_m1 = fetch(m1_ref.at[:, own_cols], mom1.at[c])
    get_m2 = fetch(m2_ref.at[:, own_cols], mom2.at[c])

    get_act.wait()
    get_proj.wait()
    partial = jnp.dot(act[...], proj[...], preferred_element_type=F32)
    part[...] = jnp.transpose(partial).astype(BF).reshape(part.shape)

    pl.semaphore_wait(barrier, len(peers))
    pl.semaphore_signal(opposite_in, inc=1, device_id=dev(zh=at(zh, 1)), device_id_type=MESH)
    pieces = [(at(x, o), pl.ds(start, count)) for o, start, count in PIECES]
    ys = [
        [go(part.at[at(y, o), p, r], y_in.at[o - 1, p, r], dev(y=at(y, o))) for o in far]
        for p, r in pieces
    ]
    cot_x = go(cot_ref.at[:, sib_cols], cot_sib, sibling)
    m1_x = go(m1_ref.at[:, sib_cols], mom1.at[c], sibling)
    m2_x = go(m2_ref.at[:, sib_cols], mom2.at[c], sibling)
    zs = []
    for (p, r), copies in zip(pieces, ys):
        for copy in copies:
            copy.wait_recv()
        total = part[y, p, r].astype(F32)
        for o in range(3):
            total += y_in[o, p, r].astype(F32)
        y_sum[p, r] = total.astype(BF)
        copies = []
        for o in far if zs else (1, 3, 2):
            if o == 2 and not zs:
                pl.semaphore_wait(opposite_in, 1)
            copies.append(go(y_sum.at[p, r], z_in.at[o - 1, p, r], dev(zh=at(zh, o))))
        zs.append(copies)

    piece = basis.shape[1]

    def rows(q):
        return proj_ref.at[pl.ds(pl.multiple_of(c * (N * piece) + q * piece, piece), piece)]

    first_sem = counter[0]
    basis_cut = [
        remote(rows(at(y, o)), quarter, dev(y=at(y, o)), first_sem) for o in (1, 2, 3)
    ]
    basis_own = held(rows(y), quarter)

    @pl.when(root)
    def _():
        for basis_part in basis_cut:
            basis_part.start()
        basis_own.start()

    handed = [None] * len(PIECES)
    grads = [[] for _ in CHUNKS]

    def add_z(i):
        p, r = pieces[i]
        for copy in zs[i]:
            copy.wait_recv()
        total = y_sum[p, r].astype(F32)
        for o in range(3):
            total += z_in[o, p, r].astype(F32)
        pj[y, p, r] = total.astype(BF)
        src = pj.at[y, p, r]
        handed[i] = [go(src, src, dev(y=at(y, o))) for o in far]
        handed[i] += [go(src, pj_sib.at[y, p, r], dev(y=at(y, o), c=1 - c)) for o in far]
        handed[i].append(go(src, pj_sib.at[y, p, r], sibling))

    def multiply(i):
        p, r = pieces[i]
        o, begin, count = PIECES[i]
        if i == 0:
            get_cot.wait()
            cot_x.wait_recv()
        for copy in handed[i]:
            copy.wait_recv()
        grad = jnp.dot(
            pj[:, p, r].reshape(N * count, -1), cot_own[...], preferred_element_type=F32
        ) + jnp.dot(
            pj_sib[:, p, r].reshape(N * count, -1), cot_sib[...], preferred_element_type=F32
        )
        lg[p, :, r] = grad.astype(BF).reshape(N, count, half)
        if o:
            for k, (start, width) in enumerate(CHUNKS):
                cols = pl.ds(start, width)
                grads[k].append(
                    go(lg.at[p, :, r, cols], g_in.at[o - 1, :, r, cols], dev(x=p))
                )

    basis_turn = remote(quarter, turned, dev(zh=at(zh, turn)))
    basis_stay = held(quarter, turned)
    basis_move = remote(turned, basis.at[y], dev(x=goal))
    basis_keep = held(turned, basis.at[y])

    def turn_basis(i):
        @pl.when(root)
        def _():
            basis_own.wait()

        @pl.when(jnp.logical_not(root))
        def _():
            basis_cut[0].wait_recv()

        @pl.when(turns)
        def _():
            basis_turn.start()

        @pl.when(jnp.logical_not(turns))
        def _():
            basis_stay.start()

    def move_basis():
        @pl.when(turns)
        def _():
            basis_turn.wait_recv()

        @pl.when(jnp.logical_not(turns))
        def _():
            basis_stay.wait()

        @pl.when(moves)
        def _():
            basis_move.start()

        @pl.when(jnp.logical_not(moves))
        def _():
            basis_keep.start()

    def share_basis():
        @pl.when(moves)
        def _():
            basis_move.wait_recv()

        @pl.when(jnp.logical_not(moves))
        def _():
            basis_keep.wait()

        return [go(basis.at[y], basis.at[y], dev(y=at(y, o))) for o in (1, 2, 3)]

    for act_on, i in (
        (add_z, 0), (add_z, 1), (multiply, 0), (add_z, 2), (multiply, 1), (add_z, 3),
        (turn_basis, 0), (multiply, 2), (multiply, 3),
    ):
        act_on(i)

    flight = [dict() for _ in CHUNKS]

    def sum_x(k):
        start, width = CHUNKS[k]
        cols = pl.ds(start, width)
        for copy in grads[k]:
            copy.wait_recv()
        total = lg[x, :, :, cols].astype(F32)
        for o in range(3):
            total += g_in[o, :, :, cols].astype(F32)
        s2[:, :, cols] = total.astype(BF)
        flight[k]["zl"] = [
            go(s2.at[at(zl, o), :, cols], zl_in.at[o - 1, :, cols], dev(zl=at(zl, o)))
            for o in (1, 2, 3)
        ]

    def step(k):
        start, width = CHUNKS[k]
        cols = pl.ds(start, width)
        f = flight[k]
        if k == 0:
            get_m1.wait()
            get_m2.wait()
            m1_x.wait_recv()
            m2_x.wait_recv()
        for copy in f["zl"]:
            copy.wait_recv()
        total = s2[zl, :, cols].astype(F32)
        for o in range(3):
            total += zl_in[o, :, cols].astype(F32)
        lowgrad = (total * grad_scale).reshape(2, 16, width)
        first, second, direction = adam(lowgrad, mom1[:, :, cols], mom2[:, :, cols])
        dirs[zl, x, :, cols] = direction.reshape(32, width)
        src = dirs.at[zl, x, :, cols]
        f["zg"] = [go(src, src, dev(zl=at(zl, o))) for o in (1, 2, 3)]
        new1[:, :, cols] = first
        new2[:, :, cols] = second

    def block(ref, k, p):
        start, width = CHUNKS[k]
        return ref.at[pl.ds(0, N), p, :, pl.ds(start, width)]

    def send_x(k):
        f = flight[k]
        for copy in f["zg"]:
            copy.wait_recv()
        src = block(dirs, k, x)
        f["xg"] = {o: go(src, src, dev(x=at(x, o))) for o in (far if k in DIRECT else (1, 3))}
        f["sib"] = [go(src, block(dirs_sib, k, x), sibling)]

    def to_sibling(k, o):
        xx = at(x, N - o)
        flight[k]["sib"].append(go(block(dirs, k, xx), block(dirs_sib, k, xx), sibling))

    def relay_x(k):
        start, width = CHUNKS[k]
        f = flight[k]
        for o in (1, 3):
            f["xg"][o].wait_recv()
            if k not in DIRECT:
                src = dirs.at[pl.ds(o - 1, 2), at(x, N - o), :, pl.ds(start, width)]
                f["xg"][4 + o] = go(src, src, dev(x=at(x, o)))
            to_sibling(k, o)

    def finish_x(k):
        f = flight[k]
        for o in (2,) if k in DIRECT else (5, 7):
            f["xg"][o].wait_recv()
        to_sibling(k, 2)

    back = (((0,), (1,)), ((), ()))
    written = []

    def update(k):
        start, width = CHUNKS[k]
        cols = pl.ds(start, width)
        if k == 0:
            for copy in basis_copies:
                copy.wait_recv()
        whole = basis[...].reshape(N * piece, -1)
        for j, (ref, core) in enumerate(((dirs, c), (dirs_sib, 1 - c))):
            if j == 1:
                for copy in flight[k]["sib"]:
                    copy.wait_recv()
            d = ref[:, :, :, cols].reshape(N * N * 32, width)
            upd[j, cols] = lax.dot_general(
                d, whole, back, preferred_element_type=F32
            ).astype(BF)
            written.append(
                fetch(
                    upd.at[j, cols],
                    up_ref.at[pl.ds(pl.multiple_of(core * half + start, 128), width)],
                )
            )

    def each(act_on):
        for k in range(len(CHUNKS)):
            act_on(k)

    each(sum_x)
    move_basis()
    each(step)
    moments_out = [
        go(new1.at[1 - c], nf_ref.at[:, own_cols], sibling),
        go(new2.at[1 - c], ns_ref.at[:, own_cols], sibling),
    ]
    written.append(fetch(new1.at[c], nf_ref.at[:, own_cols]))
    written.append(fetch(new2.at[c], ns_ref.at[:, own_cols]))
    send_x(0)
    basis_copies = share_basis()
    for k in range(1, len(CHUNKS)):
        send_x(k)
    for act_on, k in (
        (relay_x, 0), (relay_x, 1), (finish_x, 0), (update, 0), (finish_x, 1), (relay_x, 2),
        (finish_x, 2), (update, 1), (update, 2),
    ):
        act_on(k)
    assert counter[0] <= send_sems.shape[0] and counter[1] <= local_sems.shape[0]
    for copy in moments_out:
        copy.wait_recv()
    for copy in written:
        copy.wait()
    for copy in sent:
        copy.wait_send()

    @pl.when(root)
    def _():
        for basis_part in basis_cut:
            basis_part.wait_send()

    @pl.when(turns)
    def _():
        basis_turn.wait_send()

    @pl.when(moves)
    def _():
        basis_move.wait_send()


def hand_over(a_ref, b_ref, c_ref, a_out, b_out, c_out, a, b, c, sems):
    rows = c.shape[0] // 4
    trips = [(a_ref, a, a_out), (b_ref, b, b_out)]
    for i in range(4):
        part = pl.ds(i * rows, rows)
        trips.append((c_ref.at[part], c.at[part], c_out.at[part]))
    inward = [pltpu.make_async_copy(s, v, sems.at[0, i]) for i, (s, v, _) in enumerate(trips)]
    outward = [pltpu.make_async_copy(v, d, sems.at[1, i]) for i, (_, v, d) in enumerate(trips)]
    for copy in inward:
        copy.start()
    for arrive, leave in zip(inward, outward):
        arrive.wait()
        leave.start()
    for copy in outward:
        copy.wait()


def local(activations, out_cotangent, projector, first_moment, second_moment):
    tokens, features = activations.shape
    ff = out_cotangent.shape[1]
    rank = projector.shape[1]
    half = ff // 2
    width = projector.shape[0] // 2
    total_tokens = tokens * lax.axis_size("dp")
    remotes = 13 * len(PIECES) + 3 + 8 + len(CHUNKS) * (len(PIECES) - 1 + 3 + 3 + 8) + 2
    locals_ = 10 + 2 * len(CHUNKS)
    vmem = pltpu.VMEM
    scratch = [
        vmem((tokens, features), BF), vmem(projector.shape, BF),
        vmem((tokens, half), BF), vmem((tokens, half), BF),
        vmem((2, 16, half), F32), vmem((2, 16, half), F32),
        vmem((N, width // N, rank), BF), vmem((width // N, rank), BF), vmem((width // N, rank), BF),
        vmem((N, N, 32, tokens), BF), vmem((3, N, 32, tokens), BF), vmem((N, 32, tokens), BF),
        vmem((3, N, 32, tokens), BF), vmem((N, N, 32, tokens), BF), vmem((N, N, 32, tokens), BF),
        vmem((N, N, 32, half), BF), vmem((3, N, 32, half), BF),
        vmem((N, 32, half), BF), vmem((3, 32, half), BF),
        vmem((2, 16, half), F32), vmem((2, 16, half), F32),
        vmem((N, N, 32, half), BF), vmem((N, N, 32, half), BF),
        vmem((2, half, width), BF),
        pltpu.SemaphoreType.DMA((remotes,)), pltpu.SemaphoreType.DMA((remotes,)),
        pltpu.SemaphoreType.DMA((locals_,)), pltpu.SemaphoreType.REGULAR,
    ]
    anyspec = pl.BlockSpec(memory_space=pl.ANY)
    outs = (
        jax.ShapeDtypeStruct(first_moment.shape, F32),
        jax.ShapeDtypeStruct(second_moment.shape, F32),
        jax.ShapeDtypeStruct((ff, width), BF),
    )
    results = pl.pallas_call(
        functools.partial(kernel, 1.0 / math.sqrt(total_tokens)),
        out_shape=outs,
        in_specs=[anyspec] * 5,
        out_specs=(anyspec,) * 3,
        scratch_shapes=scratch,
        compiler_params=pltpu.CompilerParams(
            collective_id=0, has_side_effects=True, vmem_limit_bytes=56 * 1024 * 1024
        ),
    )(activations, out_cotangent, projector, first_moment, second_moment)
    return pl.pallas_call(
        hand_over,
        out_shape=outs,
        in_specs=[anyspec] * 3,
        out_specs=(anyspec,) * 3,
        scratch_shapes=[vmem(o.shape, o.dtype) for o in outs]
        + [pltpu.SemaphoreType.DMA((2, 6))],
        compiler_params=pltpu.CompilerParams(vmem_limit_bytes=56 * 1024 * 1024),
    )(*results)


def solution(mesh):
    placed = (P("dp", "fsdp"), P("dp", "fsdp"), P("fsdp", None), P("dp", "fsdp"), P("dp", "fsdp"))
    return jax.shard_map(
        local,
        mesh=mesh,
        in_specs=placed,
        out_specs=(P("dp", "fsdp"), P("dp", "fsdp"), P("fsdp", "dp")),
        check_vma=False,
    )
```

```python
import functools
import math

import jax
import jax.numpy as jnp
from jax import lax
from jax.experimental import pallas as pl
from jax.experimental.pallas import tpu as pltpu
from jax.sharding import PartitionSpec as P

MESH = pl.DeviceIdType.MESH
STEP = 100
BF = jnp.bfloat16
F32 = jnp.float32
CHUNKS = ((0, 256), (256, 256), (512, 384))
N = 4
PIECES = ((2, 0, 32), (1, 0, 32), (3, 0, 32), (0, 0, 32))


def adam(lowgrad, first, second):
    new_first = 0.9 * first + (1.0 - 0.9) * lowgrad
    new_second = 0.999 * second + (1.0 - 0.999) * lowgrad * lowgrad
    first_fix = 1.0 - 0.9**STEP
    second_fix = 1.0 - 0.999**STEP
    direction = new_first / first_fix / (jnp.sqrt(new_second / second_fix) + 1e-08)
    return new_first, new_second, direction.astype(BF)


def kernel(
    grad_scale, act_ref, cot_ref, proj_ref, m1_ref, m2_ref,
    nf_ref, ns_ref, up_ref,
    act, proj, cot_own, cot_sib, mom1, mom2, basis, quarter, turned,
    part, y_in, y_sum, z_in, pj, pj_sib,
    lg, g_in, s2, zl_in, new1, new2, dirs, dirs_sib, upd,
    send_sems, recv_sems, local_sems,
):
    dp, fs = lax.axis_index("dp"), lax.axis_index("fsdp")
    zl, x, c = dp // 8, (dp // 2) % 4, dp % 2
    y, zh = fs // 4, fs % 4
    half = cot_own.shape[1]

    def dev(x=x, y=y, zh=zh, zl=zl, c=c):
        return (zl * 8 + x * 2 + c, y * 4 + zh)

    def at(base, off):
        return lax.rem(base + off, N)

    sibling = dev(c=1 - c)
    root = y == zl
    turn = at(x, zl)
    goal = lax.rem(zh - x - zl + 2 * N, N)
    turns, moves = turn != 0, goal != x
    counter = [0, 0]
    sent = []

    def remote(src, dst, device, recv=None):
        i = counter[0]
        counter[0] += 1
        copy = pltpu.make_async_remote_copy(
            src_ref=src, dst_ref=dst, send_sem=send_sems.at[i],
            recv_sem=recv_sems.at[i if recv is None else recv],
            device_id=device, device_id_type=MESH,
        )
        return copy

    def go(src, dst, device):
        copy = remote(src, dst, device)
        copy.start()
        sent.append(copy)
        return copy

    def held(src, dst):
        i = counter[1]
        counter[1] += 1
        return pltpu.make_async_copy(src, dst, local_sems.at[i])

    def fetch(src, dst):
        copy = held(src, dst)
        copy.start()
        return copy

    own_cols = pl.ds(pl.multiple_of(c * half, 128), half)
    sib_cols = pl.ds(pl.multiple_of((1 - c) * half, 128), half)

    barrier = pltpu.get_barrier_semaphore()
    far = (2, 1, 3)
    peers = [dev(zh=at(zh, o)) for o in far] + [dev(y=at(y, o)) for o in far] + [sibling]
    peers += [dev(y=at(y, o), c=1 - c) for o in far]
    peers += [dev(zl=at(zl, o)) for o in far] + [dev(x=at(x, o)) for o in far]
    get_act = fetch(act_ref, act)
    get_proj = fetch(proj_ref, proj)
    for p in peers:
        pl.semaphore_signal(barrier, inc=1, device_id=p, device_id_type=MESH)

    get_cot = fetch(cot_ref.at[:, own_cols], cot_own)
    get_m1 = fetch(m1_ref.at[:, own_cols], mom1.at[c])
    get_m2 = fetch(m2_ref.at[:, own_cols], mom2.at[c])

    get_act.wait()
    get_proj.wait()
    partial = jnp.dot(act[...], proj[...], preferred_element_type=F32)
    part[...] = jnp.transpose(partial).astype(BF).reshape(part.shape)

    pl.semaphore_wait(barrier, len(peers))
    pieces = [(at(x, o), pl.ds(start, count)) for o, start, count in PIECES]
    ys = [
        [go(part.at[at(y, o), p, r], y_in.at[o - 1, p, r], dev(y=at(y, o))) for o in far]
        for p, r in pieces
    ]
    cot_x = go(cot_ref.at[:, sib_cols], cot_sib, sibling)
    m1_x = go(m1_ref.at[:, sib_cols], mom1.at[c], sibling)
    m2_x = go(m2_ref.at[:, sib_cols], mom2.at[c], sibling)
    zs = []
    for (p, r), copies in zip(pieces, ys):
        for copy in copies:
            copy.wait_recv()
        total = part[y, p, r].astype(F32)
        for o in range(3):
            total += y_in[o, p, r].astype(F32)
        y_sum[p, r] = total.astype(BF)
        zs.append([go(y_sum.at[p, r], z_in.at[o - 1, p, r], dev(zh=at(zh, o))) for o in far])

    piece = basis.shape[1]

    def rows(q):
        return proj_ref.at[pl.ds(pl.multiple_of(c * (N * piece) + q * piece, piece), piece)]

    first_sem = counter[0]
    basis_cut = [
        remote(rows(at(y, o)), quarter, dev(y=at(y, o)), first_sem) for o in (1, 2, 3)
    ]
    basis_own = held(rows(y), quarter)

    @pl.when(root)
    def _():
        for basis_part in basis_cut:
            basis_part.start()
        basis_own.start()

    handed = [None] * len(PIECES)
    grads = [[] for _ in CHUNKS]

    def add_z(i):
        p, r = pieces[i]
        for copy in zs[i]:
            copy.wait_recv()
        total = y_sum[p, r].astype(F32)
        for o in range(3):
            total += z_in[o, p, r].astype(F32)
        pj[y, p, r] = total.astype(BF)
        src = pj.at[y, p, r]
        handed[i] = [go(src, src, dev(y=at(y, o))) for o in far]
        handed[i] += [go(src, pj_sib.at[y, p, r], dev(y=at(y, o), c=1 - c)) for o in far]
        handed[i].append(go(src, pj_sib.at[y, p, r], sibling))

    def multiply(i):
        p, r = pieces[i]
        o, begin, count = PIECES[i]
        if i == 0:
            get_cot.wait()
            cot_x.wait_recv()
        for copy in handed[i]:
            copy.wait_recv()
        grad = jnp.dot(
            pj[:, p, r].reshape(N * count, -1), cot_own[...], preferred_element_type=F32
        ) + jnp.dot(
            pj_sib[:, p, r].reshape(N * count, -1), cot_sib[...], preferred_element_type=F32
        )
        lg[p, :, r] = grad.astype(BF).reshape(N, count, half)
        if o:
            for k, (start, width) in enumerate(CHUNKS):
                cols = pl.ds(start, width)
                grads[k].append(
                    go(lg.at[p, :, r, cols], g_in.at[o - 1, :, r, cols], dev(x=p))
                )

    basis_turn = remote(quarter, turned, dev(zh=at(zh, turn)))
    basis_stay = held(quarter, turned)
    basis_move = remote(turned, basis.at[y], dev(x=goal))
    basis_keep = held(turned, basis.at[y])

    def turn_basis(i):
        @pl.when(root)
        def _():
            basis_own.wait()

        @pl.when(jnp.logical_not(root))
        def _():
            basis_cut[0].wait_recv()

        @pl.when(turns)
        def _():
            basis_turn.start()

        @pl.when(jnp.logical_not(turns))
        def _():
            basis_stay.start()

    def move_basis():
        @pl.when(turns)
        def _():
            basis_turn.wait_recv()

        @pl.when(jnp.logical_not(turns))
        def _():
            basis_stay.wait()

        @pl.when(moves)
        def _():
            basis_move.start()

        @pl.when(jnp.logical_not(moves))
        def _():
            basis_keep.start()

    def share_basis():
        @pl.when(moves)
        def _():
            basis_move.wait_recv()

        @pl.when(jnp.logical_not(moves))
        def _():
            basis_keep.wait()

        return [go(basis.at[y], basis.at[y], dev(y=at(y, o))) for o in (1, 2, 3)]

    for act_on, i in (
        (add_z, 0), (add_z, 1), (multiply, 0), (add_z, 2), (multiply, 1), (add_z, 3),
        (turn_basis, 0), (multiply, 2), (multiply, 3),
    ):
        act_on(i)

    flight = [dict() for _ in CHUNKS]

    def sum_x(k):
        start, width = CHUNKS[k]
        cols = pl.ds(start, width)
        for copy in grads[k]:
            copy.wait_recv()
        total = lg[x, :, :, cols].astype(F32)
        for o in range(3):
            total += g_in[o, :, :, cols].astype(F32)
        s2[:, :, cols] = total.astype(BF)
        flight[k]["zl"] = [
            go(s2.at[at(zl, o), :, cols], zl_in.at[o - 1, :, cols], dev(zl=at(zl, o)))
            for o in (1, 2, 3)
        ]

    def step(k):
        start, width = CHUNKS[k]
        cols = pl.ds(start, width)
        f = flight[k]
        if k == 0:
            get_m1.wait()
            get_m2.wait()
            m1_x.wait_recv()
            m2_x.wait_recv()
        for copy in f["zl"]:
            copy.wait_recv()
        total = s2[zl, :, cols].astype(F32)
        for o in range(3):
            total += zl_in[o, :, cols].astype(F32)
        lowgrad = (total * grad_scale).reshape(2, 16, width)
        first, second, direction = adam(lowgrad, mom1[:, :, cols], mom2[:, :, cols])
        dirs[zl, x, :, cols] = direction.reshape(32, width)
        src = dirs.at[zl, x, :, cols]
        f["zg"] = [go(src, src, dev(zl=at(zl, o))) for o in (1, 2, 3)]
        new1[:, :, cols] = first
        new2[:, :, cols] = second

    def block(ref, k, p):
        start, width = CHUNKS[k]
        return ref.at[pl.ds(0, N), p, :, pl.ds(start, width)]

    def send_x(k):
        f = flight[k]
        for copy in f["zg"]:
            copy.wait_recv()
        src = block(dirs, k, x)
        f["xg"] = {o: go(src, src, dev(x=at(x, o))) for o in far}
        f["sib"] = [go(src, block(dirs_sib, k, x), sibling)]

    def to_sibling(k, o):
        xx = at(x, N - o)
        flight[k]["sib"].append(go(block(dirs, k, xx), block(dirs_sib, k, xx), sibling))

    def relay_x(k):
        f = flight[k]
        for o in (1, 3):
            f["xg"][o].wait_recv()
            to_sibling(k, o)

    def finish_x(k):
        flight[k]["xg"][2].wait_recv()
        to_sibling(k, 2)

    back = (((0,), (1,)), ((), ()))
    written = []

    def update(k):
        start, width = CHUNKS[k]
        cols = pl.ds(start, width)
        if k == 0:
            for copy in basis_copies:
                copy.wait_recv()
        whole = basis[...].reshape(N * piece, -1)
        for j, (ref, core) in enumerate(((dirs, c), (dirs_sib, 1 - c))):
            if j == 1:
                for copy in flight[k]["sib"]:
                    copy.wait_recv()
            d = ref[:, :, :, cols].reshape(N * N * 32, width)
            upd[j, cols] = lax.dot_general(
                d, whole, back, preferred_element_type=F32
            ).astype(BF)
            written.append(
                fetch(
                    upd.at[j, cols],
                    up_ref.at[pl.ds(pl.multiple_of(core * half + start, 128), width)],
                )
            )

    def each(act_on):
        for k in range(len(CHUNKS)):
            act_on(k)

    each(sum_x)
    move_basis()
    each(step)
    moments_out = [
        go(new1.at[1 - c], nf_ref.at[:, own_cols], sibling),
        go(new2.at[1 - c], ns_ref.at[:, own_cols], sibling),
    ]
    written.append(fetch(new1.at[c], nf_ref.at[:, own_cols]))
    written.append(fetch(new2.at[c], ns_ref.at[:, own_cols]))
    send_x(0)
    basis_copies = share_basis()
    for k in range(1, len(CHUNKS)):
        send_x(k)
    for act_on, k in (
        (relay_x, 0), (relay_x, 1), (finish_x, 0), (update, 0), (finish_x, 1), (relay_x, 2),
        (finish_x, 2), (update, 1), (update, 2),
    ):
        act_on(k)
    assert counter[0] <= send_sems.shape[0] and counter[1] <= local_sems.shape[0]
    for copy in moments_out:
        copy.wait_recv()
    for copy in written:
        copy.wait()
    for copy in sent:
        copy.wait_send()

    @pl.when(root)
    def _():
        for basis_part in basis_cut:
            basis_part.wait_send()

    @pl.when(turns)
    def _():
        basis_turn.wait_send()

    @pl.when(moves)
    def _():
        basis_move.wait_send()


def hand_over(a_ref, b_ref, c_ref, a_out, b_out, c_out, a, b, c, sems):
    rows = c.shape[0] // 4
    trips = [(a_ref, a, a_out), (b_ref, b, b_out)]
    for i in range(4):
        part = pl.ds(i * rows, rows)
        trips.append((c_ref.at[part], c.at[part], c_out.at[part]))
    inward = [pltpu.make_async_copy(s, v, sems.at[0, i]) for i, (s, v, _) in enumerate(trips)]
    outward = [pltpu.make_async_copy(v, d, sems.at[1, i]) for i, (_, v, d) in enumerate(trips)]
    for copy in inward:
        copy.start()
    for arrive, leave in zip(inward, outward):
        arrive.wait()
        leave.start()
    for copy in outward:
        copy.wait()


def local(activations, out_cotangent, projector, first_moment, second_moment):
    tokens, features = activations.shape
    ff = out_cotangent.shape[1]
    rank = projector.shape[1]
    half = ff // 2
    width = projector.shape[0] // 2
    total_tokens = tokens * lax.axis_size("dp")
    remotes = 13 * len(PIECES) + 3 + 8 + len(CHUNKS) * (len(PIECES) - 1 + 3 + 3 + 7) + 2
    locals_ = 10 + 2 * len(CHUNKS)
    vmem = pltpu.VMEM
    scratch = [
        vmem((tokens, features), BF), vmem(projector.shape, BF),
        vmem((tokens, half), BF), vmem((tokens, half), BF),
        vmem((2, 16, half), F32), vmem((2, 16, half), F32),
        vmem((N, width // N, rank), BF), vmem((width // N, rank), BF), vmem((width // N, rank), BF),
        vmem((N, N, 32, tokens), BF), vmem((3, N, 32, tokens), BF), vmem((N, 32, tokens), BF),
        vmem((3, N, 32, tokens), BF), vmem((N, N, 32, tokens), BF), vmem((N, N, 32, tokens), BF),
        vmem((N, N, 32, half), BF), vmem((3, N, 32, half), BF),
        vmem((N, 32, half), BF), vmem((3, 32, half), BF),
        vmem((2, 16, half), F32), vmem((2, 16, half), F32),
        vmem((N, N, 32, half), BF), vmem((N, N, 32, half), BF),
        vmem((2, half, width), BF),
        pltpu.SemaphoreType.DMA((remotes,)), pltpu.SemaphoreType.DMA((remotes,)),
        pltpu.SemaphoreType.DMA((locals_,)),
    ]
    anyspec = pl.BlockSpec(memory_space=pl.ANY)
    outs = (
        jax.ShapeDtypeStruct(first_moment.shape, F32),
        jax.ShapeDtypeStruct(second_moment.shape, F32),
        jax.ShapeDtypeStruct((ff, width), BF),
    )
    results = pl.pallas_call(
        functools.partial(kernel, 1.0 / math.sqrt(total_tokens)),
        out_shape=outs,
        in_specs=[anyspec] * 5,
        out_specs=(anyspec,) * 3,
        scratch_shapes=scratch,
        compiler_params=pltpu.CompilerParams(
            collective_id=0, has_side_effects=True, vmem_limit_bytes=56 * 1024 * 1024
        ),
    )(activations, out_cotangent, projector, first_moment, second_moment)
    return pl.pallas_call(
        hand_over,
        out_shape=outs,
        in_specs=[anyspec] * 3,
        out_specs=(anyspec,) * 3,
        scratch_shapes=[vmem(o.shape, o.dtype) for o in outs]
        + [pltpu.SemaphoreType.DMA((2, 6))],
        compiler_params=pltpu.CompilerParams(vmem_limit_bytes=56 * 1024 * 1024),
    )(*results)


def solution(mesh):
    placed = (P("dp", "fsdp"), P("dp", "fsdp"), P("fsdp", None), P("dp", "fsdp"), P("dp", "fsdp"))
    return jax.shard_map(
        local,
        mesh=mesh,
        in_specs=placed,
        out_specs=(P("dp", "fsdp"), P("dp", "fsdp"), P("fsdp", "dp")),
        check_vma=False,
    )
```

```python
import functools
import math

import jax
import jax.numpy as jnp
from jax import lax
from jax.experimental import pallas as pl
from jax.experimental.pallas import tpu as pltpu
from jax.sharding import PartitionSpec as P

MESH = pl.DeviceIdType.MESH
STEP = 100
BF = jnp.bfloat16
F32 = jnp.float32
CHUNKS = ((0, 256), (256, 256), (512, 384))
N = 4
PIECES = ((2, 0, 32), (1, 0, 32), (3, 0, 32), (0, 0, 32))


def adam(lowgrad, first, second):
    new_first = 0.9 * first + (1.0 - 0.9) * lowgrad
    new_second = 0.999 * second + (1.0 - 0.999) * lowgrad * lowgrad
    first_fix = 1.0 - 0.9**STEP
    second_fix = 1.0 - 0.999**STEP
    direction = new_first / first_fix / (jnp.sqrt(new_second / second_fix) + 1e-08)
    return new_first, new_second, direction.astype(BF)


def kernel(
    grad_scale, act_ref, cot_ref, proj_ref, m1_ref, m2_ref,
    nf_ref, ns_ref, up_ref,
    act, proj, cot_own, cot_sib, mom1, mom2, basis, quarter, turned,
    part, y_in, y_sum, z_in, pj, pj_sib,
    lg, g_in, s2, zl_in, new1, new2, dirs, dirs_sib, upd,
    send_sems, recv_sems, local_sems,
):
    dp, fs = lax.axis_index("dp"), lax.axis_index("fsdp")
    zl, x, c = dp // 8, (dp // 2) % 4, dp % 2
    y, zh = fs // 4, fs % 4
    half = cot_own.shape[1]

    def dev(x=x, y=y, zh=zh, zl=zl, c=c):
        return (zl * 8 + x * 2 + c, y * 4 + zh)

    def at(base, off):
        return lax.rem(base + off, N)

    sibling = dev(c=1 - c)
    root = y == zl
    turn = at(x, zl)
    goal = lax.rem(zh - x - zl + 2 * N, N)
    turns, moves = turn != 0, goal != x
    counter = [0, 0]
    sent = []

    def remote(src, dst, device, recv=None):
        i = counter[0]
        counter[0] += 1
        copy = pltpu.make_async_remote_copy(
            src_ref=src, dst_ref=dst, send_sem=send_sems.at[i],
            recv_sem=recv_sems.at[i if recv is None else recv],
            device_id=device, device_id_type=MESH,
        )
        return copy

    def go(src, dst, device):
        copy = remote(src, dst, device)
        copy.start()
        sent.append(copy)
        return copy

    def held(src, dst):
        i = counter[1]
        counter[1] += 1
        return pltpu.make_async_copy(src, dst, local_sems.at[i])

    def fetch(src, dst):
        copy = held(src, dst)
        copy.start()
        return copy

    own_cols = pl.ds(pl.multiple_of(c * half, 128), half)
    sib_cols = pl.ds(pl.multiple_of((1 - c) * half, 128), half)

    barrier = pltpu.get_barrier_semaphore()
    far = (2, 1, 3)
    peers = [dev(zh=at(zh, o)) for o in far] + [dev(y=at(y, o)) for o in far] + [sibling]
    peers += [dev(y=at(y, o), c=1 - c) for o in far]
    peers += [dev(zl=at(zl, o)) for o in far] + [dev(x=at(x, o)) for o in far]
    get_act = fetch(act_ref, act)
    get_proj = fetch(proj_ref, proj)
    for p in peers:
        pl.semaphore_signal(barrier, inc=1, device_id=p, device_id_type=MESH)

    get_cot = fetch(cot_ref.at[:, own_cols], cot_own)
    get_m1 = fetch(m1_ref.at[:, own_cols], mom1.at[c])
    get_m2 = fetch(m2_ref.at[:, own_cols], mom2.at[c])

    get_act.wait()
    get_proj.wait()
    partial = jnp.dot(act[...], proj[...], preferred_element_type=F32)
    part[...] = jnp.transpose(partial).astype(BF).reshape(part.shape)

    pl.semaphore_wait(barrier, len(peers))
    pieces = [(at(x, o), pl.ds(start, count)) for o, start, count in PIECES]
    ys = [
        [go(part.at[at(y, o), p, r], y_in.at[o - 1, p, r], dev(y=at(y, o))) for o in far]
        for p, r in pieces
    ]
    cot_x = go(cot_ref.at[:, sib_cols], cot_sib, sibling)
    m1_x = go(m1_ref.at[:, sib_cols], mom1.at[c], sibling)
    m2_x = go(m2_ref.at[:, sib_cols], mom2.at[c], sibling)
    zs = []
    for (p, r), copies in zip(pieces, ys):
        for copy in copies:
            copy.wait_recv()
        total = part[y, p, r].astype(F32)
        for o in range(3):
            total += y_in[o, p, r].astype(F32)
        y_sum[p, r] = total.astype(BF)
        zs.append([go(y_sum.at[p, r], z_in.at[o - 1, p, r], dev(zh=at(zh, o))) for o in far])

    piece = basis.shape[1]

    def rows(q):
        return proj_ref.at[pl.ds(pl.multiple_of(c * (N * piece) + q * piece, piece), piece)]

    first_sem = counter[0]
    basis_cut = [
        remote(rows(at(y, o)), quarter, dev(y=at(y, o)), first_sem) for o in (1, 2, 3)
    ]
    basis_own = held(rows(y), quarter)

    @pl.when(root)
    def _():
        for basis_part in basis_cut:
            basis_part.start()
        basis_own.start()

    handed = [None] * len(PIECES)
    grads = [[] for _ in CHUNKS]

    def add_z(i):
        p, r = pieces[i]
        for copy in zs[i]:
            copy.wait_recv()
        total = y_sum[p, r].astype(F32)
        for o in range(3):
            total += z_in[o, p, r].astype(F32)
        pj[y, p, r] = total.astype(BF)
        src = pj.at[y, p, r]
        handed[i] = []
        for o in far:
            handed[i].append(go(src, pj_sib.at[y, p, r], dev(y=at(y, o), c=1 - c)))
            handed[i].append(go(src, src, dev(y=at(y, o))))
        handed[i].append(go(src, pj_sib.at[y, p, r], sibling))

    def multiply(i):
        p, r = pieces[i]
        o, begin, count = PIECES[i]
        if i == 0:
            get_cot.wait()
            cot_x.wait_recv()
        for copy in handed[i]:
            copy.wait_recv()
        grad = jnp.dot(
            pj[:, p, r].reshape(N * count, -1), cot_own[...], preferred_element_type=F32
        ) + jnp.dot(
            pj_sib[:, p, r].reshape(N * count, -1), cot_sib[...], preferred_element_type=F32
        )
        lg[p, :, r] = grad.astype(BF).reshape(N, count, half)
        if o:
            for k, (start, width) in enumerate(CHUNKS):
                cols = pl.ds(start, width)
                grads[k].append(
                    go(lg.at[p, :, r, cols], g_in.at[o - 1, :, r, cols], dev(x=p))
                )

    basis_turn = remote(quarter, turned, dev(zh=at(zh, turn)))
    basis_stay = held(quarter, turned)
    basis_move = remote(turned, basis.at[y], dev(x=goal))
    basis_keep = held(turned, basis.at[y])

    def turn_basis(i):
        @pl.when(root)
        def _():
            basis_own.wait()

        @pl.when(jnp.logical_not(root))
        def _():
            basis_cut[0].wait_recv()

        @pl.when(turns)
        def _():
            basis_turn.start()

        @pl.when(jnp.logical_not(turns))
        def _():
            basis_stay.start()

    def move_basis():
        @pl.when(turns)
        def _():
            basis_turn.wait_recv()

        @pl.when(jnp.logical_not(turns))
        def _():
            basis_stay.wait()

        @pl.when(moves)
        def _():
            basis_move.start()

        @pl.when(jnp.logical_not(moves))
        def _():
            basis_keep.start()

    def share_basis():
        @pl.when(moves)
        def _():
            basis_move.wait_recv()

        @pl.when(jnp.logical_not(moves))
        def _():
            basis_keep.wait()

        return [go(basis.at[y], basis.at[y], dev(y=at(y, o))) for o in (1, 2, 3)]

    for act_on, i in (
        (add_z, 0), (add_z, 1), (multiply, 0), (add_z, 2), (multiply, 1), (add_z, 3),
        (turn_basis, 0), (multiply, 2), (multiply, 3),
    ):
        act_on(i)

    flight = [dict() for _ in CHUNKS]

    def sum_x(k):
        start, width = CHUNKS[k]
        cols = pl.ds(start, width)
        for copy in grads[k]:
            copy.wait_recv()
        total = lg[x, :, :, cols].astype(F32)
        for o in range(3):
            total += g_in[o, :, :, cols].astype(F32)
        s2[:, :, cols] = total.astype(BF)
        flight[k]["zl"] = [
            go(s2.at[at(zl, o), :, cols], zl_in.at[o - 1, :, cols], dev(zl=at(zl, o)))
            for o in far
        ]

    def step(k):
        start, width = CHUNKS[k]
        cols = pl.ds(start, width)
        f = flight[k]
        if k == 0:
            get_m1.wait()
            get_m2.wait()
            m1_x.wait_recv()
            m2_x.wait_recv()
        for copy in f["zl"]:
            copy.wait_recv()
        total = s2[zl, :, cols].astype(F32)
        for o in range(3):
            total += zl_in[o, :, cols].astype(F32)
        lowgrad = (total * grad_scale).reshape(2, 16, width)
        first, second, direction = adam(lowgrad, mom1[:, :, cols], mom2[:, :, cols])
        dirs[zl, x, :, cols] = direction.reshape(32, width)
        src = dirs.at[zl, x, :, cols]
        f["zg"] = [go(src, src, dev(zl=at(zl, o))) for o in far]
        new1[:, :, cols] = first
        new2[:, :, cols] = second

    def block(ref, k, p):
        start, width = CHUNKS[k]
        return ref.at[pl.ds(0, N), p, :, pl.ds(start, width)]

    def send_x(k):
        f = flight[k]
        for copy in f["zg"]:
            copy.wait_recv()
        src = block(dirs, k, x)
        f["xg"] = {o: go(src, src, dev(x=at(x, o))) for o in far}
        f["sib"] = [go(src, block(dirs_sib, k, x), sibling)]

    def to_sibling(k, o):
        xx = at(x, N - o)
        flight[k]["sib"].append(go(block(dirs, k, xx), block(dirs_sib, k, xx), sibling))

    def relay_x(k):
        f = flight[k]
        for o in (1, 3):
            f["xg"][o].wait_recv()
            to_sibling(k, o)

    def finish_x(k):
        flight[k]["xg"][2].wait_recv()
        to_sibling(k, 2)

    back = (((0,), (1,)), ((), ()))
    written = []

    def update(k):
        start, width = CHUNKS[k]
        cols = pl.ds(start, width)
        if k == 0:
            for copy in basis_copies:
                copy.wait_recv()
        whole = basis[...].reshape(N * piece, -1)
        for j, (ref, core) in enumerate(((dirs, c), (dirs_sib, 1 - c))):
            if j == 1:
                for copy in flight[k]["sib"]:
                    copy.wait_recv()
            d = ref[:, :, :, cols].reshape(N * N * 32, width)
            upd[j, cols] = lax.dot_general(
                d, whole, back, preferred_element_type=F32
            ).astype(BF)
            written.append(
                fetch(
                    upd.at[j, cols],
                    up_ref.at[pl.ds(pl.multiple_of(core * half + start, 128), width)],
                )
            )

    def each(act_on):
        for k in range(len(CHUNKS)):
            act_on(k)

    each(sum_x)
    move_basis()
    each(step)
    moments_out = [
        go(new1.at[1 - c], nf_ref.at[:, own_cols], sibling),
        go(new2.at[1 - c], ns_ref.at[:, own_cols], sibling),
    ]
    written.append(fetch(new1.at[c], nf_ref.at[:, own_cols]))
    written.append(fetch(new2.at[c], ns_ref.at[:, own_cols]))
    send_x(0)
    basis_copies = share_basis()
    for k in range(1, len(CHUNKS)):
        send_x(k)
    for act_on, k in (
        (relay_x, 0), (relay_x, 1), (finish_x, 0), (update, 0), (finish_x, 1), (relay_x, 2),
        (finish_x, 2), (update, 1), (update, 2),
    ):
        act_on(k)
    assert counter[0] <= send_sems.shape[0] and counter[1] <= local_sems.shape[0]
    for copy in moments_out:
        copy.wait_recv()
    for copy in written:
        copy.wait()
    for copy in sent:
        copy.wait_send()

    @pl.when(root)
    def _():
        for basis_part in basis_cut:
            basis_part.wait_send()

    @pl.when(turns)
    def _():
        basis_turn.wait_send()

    @pl.when(moves)
    def _():
        basis_move.wait_send()


def hand_over(a_ref, b_ref, c_ref, a_out, b_out, c_out, a, b, c, sems):
    rows = c.shape[0] // 4
    trips = [(a_ref, a, a_out), (b_ref, b, b_out)]
    for i in range(4):
        part = pl.ds(i * rows, rows)
        trips.append((c_ref.at[part], c.at[part], c_out.at[part]))
    inward = [pltpu.make_async_copy(s, v, sems.at[0, i]) for i, (s, v, _) in enumerate(trips)]
    outward = [pltpu.make_async_copy(v, d, sems.at[1, i]) for i, (_, v, d) in enumerate(trips)]
    for copy in inward:
        copy.start()
    for arrive, leave in zip(inward, outward):
        arrive.wait()
        leave.start()
    for copy in outward:
        copy.wait()


def local(activations, out_cotangent, projector, first_moment, second_moment):
    tokens, features = activations.shape
    ff = out_cotangent.shape[1]
    rank = projector.shape[1]
    half = ff // 2
    width = projector.shape[0] // 2
    total_tokens = tokens * lax.axis_size("dp")
    remotes = 13 * len(PIECES) + 3 + 8 + len(CHUNKS) * (len(PIECES) - 1 + 3 + 3 + 7) + 2
    locals_ = 10 + 2 * len(CHUNKS)
    vmem = pltpu.VMEM
    scratch = [
        vmem((tokens, features), BF), vmem(projector.shape, BF),
        vmem((tokens, half), BF), vmem((tokens, half), BF),
        vmem((2, 16, half), F32), vmem((2, 16, half), F32),
        vmem((N, width // N, rank), BF), vmem((width // N, rank), BF), vmem((width // N, rank), BF),
        vmem((N, N, 32, tokens), BF), vmem((3, N, 32, tokens), BF), vmem((N, 32, tokens), BF),
        vmem((3, N, 32, tokens), BF), vmem((N, N, 32, tokens), BF), vmem((N, N, 32, tokens), BF),
        vmem((N, N, 32, half), BF), vmem((3, N, 32, half), BF),
        vmem((N, 32, half), BF), vmem((3, 32, half), BF),
        vmem((2, 16, half), F32), vmem((2, 16, half), F32),
        vmem((N, N, 32, half), BF), vmem((N, N, 32, half), BF),
        vmem((2, half, width), BF),
        pltpu.SemaphoreType.DMA((remotes,)), pltpu.SemaphoreType.DMA((remotes,)),
        pltpu.SemaphoreType.DMA((locals_,)),
    ]
    anyspec = pl.BlockSpec(memory_space=pl.ANY)
    outs = (
        jax.ShapeDtypeStruct(first_moment.shape, F32),
        jax.ShapeDtypeStruct(second_moment.shape, F32),
        jax.ShapeDtypeStruct((ff, width), BF),
    )
    results = pl.pallas_call(
        functools.partial(kernel, 1.0 / math.sqrt(total_tokens)),
        out_shape=outs,
        in_specs=[anyspec] * 5,
        out_specs=(anyspec,) * 3,
        scratch_shapes=scratch,
        compiler_params=pltpu.CompilerParams(
            collective_id=0, has_side_effects=True, vmem_limit_bytes=56 * 1024 * 1024
        ),
    )(activations, out_cotangent, projector, first_moment, second_moment)
    return pl.pallas_call(
        hand_over,
        out_shape=outs,
        in_specs=[anyspec] * 3,
        out_specs=(anyspec,) * 3,
        scratch_shapes=[vmem(o.shape, o.dtype) for o in outs]
        + [pltpu.SemaphoreType.DMA((2, 6))],
        compiler_params=pltpu.CompilerParams(vmem_limit_bytes=56 * 1024 * 1024),
    )(*results)


def solution(mesh):
    placed = (P("dp", "fsdp"), P("dp", "fsdp"), P("fsdp", None), P("dp", "fsdp"), P("dp", "fsdp"))
    return jax.shard_map(
        local,
        mesh=mesh,
        in_specs=placed,
        out_specs=(P("dp", "fsdp"), P("dp", "fsdp"), P("fsdp", "dp")),
        check_vma=False,
    )
```
